32 devices in a mesh: sub: 8 (over z, y), mem: 4 (over x, core).
Axes of the slice: x: 2, y: 2, z: 4, core: 2. Of those that a mesh axis runs over, the one named last changes fastest.
Arguments:
- static_control: float32 [4, 4, 64, 1536], P('mem', None, 'sub'), may hold values from -6 to 6
- alpha_field: float32 [4, 4, 64, 1536], P('mem', None, 'sub'), may hold values from -6 to 6
- perturbations: bfloat16 [4, 4, 4, 64, 1536], P('mem', None, None, 'sub'), may hold values from -6 to 6
- static_scale: float32 [4, 4], P('mem'), may hold values from 0.5 to 2
- length_x: float32 [4], replicated, may hold values from 0.5 to 1
- length_y: float32 [4], replicated, may hold values from 2 to 16
- lengths: int32 [8], replicated, may hold values from 1 to 8, 48 in all
Outputs:
- increment: float32 [4, 4, 64, 1536], P('mem', None, 'sub')
The draws below stay inside these ranges and needn't reach their ends.
Inputs may be any that keep to these rules, and one draw needn't show every extreme that they name: lengths[d] is the number of grid rows of subdomain d; they sum to 48 and the largest is exactly 8.
All inputs are finite; a program needn't handle non-finite values.
Results may differ from the reference program's by a relative error of at most 0.0003.
Values sent between devices are 32-bit elements; how exact they have to be, the bound alone decides.
A program may use at most 64 MiB of HBM per device.

```python
import math
import jax
import jax.numpy as jnp
import numpy as np
from jax import lax

NV = 4
NX = 1536
L = 4
RMAX = 8
NY = 48
NYP = 64
MEMBERS = 4
N_SUB = 8


def levels(rng, extent, pieces, least, largest):
    level, own = 1.0, jax.random.fold_in(rng, 6)
    for axis_at, shards_of in pieces:
        heights = jnp.exp(jax.random.uniform(jax.random.fold_in(own, axis_at), (shards_of,), jnp.float32, least / len(pieces), largest / len(pieces)))
        level = level * jnp.repeat(heights, extent[axis_at] // shards_of).reshape([-1 if axis == axis_at else 1 for axis in range(len(extent))])
    return level


def split_up(count, total, bound, lean):
    loads = [(1 << 20) // math.isqrt(grade ** lean) + 1 for grade in range(2, count + 1)]
    spare, given = total - bound - (count - 1), [1] * (count - 1)
    while spare > 0:
        free = [i for i in range(count - 1) if given[i] < bound]
        whole, remaining = sum([loads[i] for i in free]), spare
        for i in free:
            more = min(bound - given[i], max(1, remaining * loads[i] // whole), spare)
            given[i] = given[i] + more
            spare = spare - more
    return np.array([bound] + given)


def uneven_parts(key, count, total, bound, lean):
    if count == 2:
        one = jax.random.randint(key, (), max(1, total - bound), min(bound, total - 1) + 1)
        return jnp.stack([one, total - one])
    sizes = jnp.asarray(split_up(count, total, bound, lean), jnp.int32)
    twos = (count - 1) // 2
    donor, receiver = sizes[1:1 + 2 * twos:2], sizes[2:2 + 2 * twos:2]
    room = jnp.minimum(donor - 1, bound - receiver)
    shifted = jax.random.randint(jax.random.fold_in(key, 1), (twos,), 0, 1 << 20) % (room + 1)
    sizes = sizes.at[1:1 + 2 * twos:2].set(donor - shifted).at[2:2 + 2 * twos:2].set(receiver + shifted)
    return sizes[jax.random.permutation(jax.random.fold_in(key, 2), count)]


def normal_values(stream_key, shape, deviation, limit, shards=(), kind=jnp.bfloat16):
    drawn = deviation * jax.random.normal(stream_key, shape, jnp.float32)
    if shards:
        drawn = drawn * levels(stream_key, shape, shards, -0.22, 0.18)
    return jnp.clip(drawn, -limit, limit).astype(kind)


def setup_inputs(seed: int = 0) -> dict:
    streams_of = jax.random.split(jax.random.key(seed), 8)
    static_control = normal_values(streams_of[0], (NV, L, NYP, NX), 1.0, 6.0, ((0, 4), (2, 8)), jnp.float32)
    alpha_field = normal_values(streams_of[1], (MEMBERS, L, NYP, NX), 1.0, 6.0, ((0, 4), (2, 8)), jnp.float32)
    perturbations = normal_values(streams_of[2], (MEMBERS, NV, L, NYP, NX), 1.0, 6.0, ((0, 4), (3, 8)))
    static_scale = jnp.clip(jnp.exp(math.log(2.0) - 1.3862944 * jax.random.uniform(streams_of[3], (NV, L), jnp.float32) ** levels(streams_of[3], (NV, L), ((0, 4),), -0.2, 0.2)), 0.5, 2.0)
    length_x = jnp.clip(jnp.exp(jax.random.uniform(streams_of[4], (L,), jnp.float32, math.log(0.5), math.log(1.0))), 0.5, 1.0)
    length_y = jnp.clip(jnp.exp(jax.random.uniform(streams_of[5], (L,), jnp.float32, math.log(2.0), math.log(16.0))), 2.0, 16.0)
    lengths = uneven_parts(streams_of[6], N_SUB, NY, RMAX, 2).astype(jnp.int32)
    return dict(static_control=static_control, alpha_field=alpha_field, perturbations=perturbations, static_scale=static_scale, length_x=length_x, length_y=length_y, lengths=lengths)


def cascade(values, length_scale):
    decays = jnp.exp(-1.0 / length_scale)[None, :, None]

    def forward(series):
        moved = jnp.moveaxis(series, -1, 0)

        def advance(states, entry):
            finals = []
            current = entry
            for section_idx in range(4):
                current = (1.0 - decays) * current + decays * states[section_idx]
                finals.append(current)
            return (tuple(finals), current)
        zero_state = tuple((jnp.zeros(moved.shape[1:], jnp.float32) for section_idx in range(4)))
        unused, result = lax.scan(advance, zero_state, moved)
        return jnp.moveaxis(result, 0, -1)
    ahead = forward(values)
    return jnp.flip(forward(jnp.flip(ahead, -1)), -1)

def row_index(lengths, rows_max, row_total):
    starts = (jnp.cumsum(lengths) - lengths).astype(jnp.int32)
    compact = jnp.arange(row_total, dtype=jnp.int32)
    owners = (lax.optimization_barrier(jnp.sum((starts[None, :] <= compact[:, None]).astype(jnp.int32), axis=1)) - 1).astype(jnp.int32)
    chosen = (owners[:, None] == jnp.arange(lengths.shape[0], dtype=jnp.int32)[None, :]).astype(jnp.int32)
    first_row = lax.optimization_barrier(jnp.sum(chosen * starts[None, :], axis=1)).astype(jnp.int32)
    return (owners * rows_max + compact - first_row).astype(jnp.int32)

def reference(static_control, alpha_field, perturbations, static_scale, length_x, length_y, lengths):
    positions = row_index(lengths, RMAX, NY)
    row_valid = (jnp.arange(RMAX, dtype=jnp.int32)[None, :] < lengths[:, None]).reshape(-1).astype(jnp.float32)
    fields = jnp.concatenate([static_control, alpha_field], 0) * row_valid[None, None, :, None]
    along_x = cascade(fields, length_x)
    gathered = jnp.take(along_x, positions, axis=2)
    along_y = jnp.moveaxis(cascade(jnp.moveaxis(gathered, 2, 3), length_y), 3, 2)
    scaled = along_y * jnp.sqrt(length_x * length_y)[None, :, None, None]
    placed = jnp.zeros(fields.shape, jnp.float32).at[:, :, positions, :].set(scaled)
    static_part = placed[:NV] * static_scale[:, :, None, None]
    member_fields = placed[NV:]

    def accumulate(member_idx, running):
        return running + perturbations[member_idx].astype(jnp.float32) * member_fields[member_idx][None]
    ensemble = lax.fori_loop(0, MEMBERS, accumulate, jnp.zeros(static_part.shape, jnp.float32))
    return static_part + ensemble * (1.0 / math.sqrt(MEMBERS))
```

```python
import functools
import math

import jax
import jax.numpy as jnp
from jax import lax
from jax.experimental import pallas as pl
from jax.experimental.pallas import tpu as pltpu
from jax.sharding import PartitionSpec as P

ROWS_DEV = 6


def recurse(values, length_scale, reverse):
    full_shape = values.shape
    line_len = full_shape[-1]
    block_len = 128 if line_len % 128 == 0 else line_len
    block_count = line_len // block_len
    if reverse:
        values = jnp.flip(values, -1)
    offsets = jnp.arange(block_len, dtype=jnp.float32)
    lagged = offsets[:, None] - offsets[None, :]
    inverse = 1.0 / length_scale
    decays = jnp.exp(-inverse)
    kernel = jnp.where(
        lagged[None] >= 0.0,
        (1.0 - decays)[:, None, None]
        * jnp.exp(-jnp.maximum(lagged, 0.0)[None] * inverse[:, None, None]),
        0.0,
    )
    carry_w = jnp.exp(-(offsets[None, :] + 1.0) * inverse[:, None])
    powers = [kernel]
    for power_idx in range(3):
        powers.append(
            jnp.einsum("lij,ljk->lik", powers[-1], kernel, precision=lax.Precision.HIGHEST)
        )
    carried = [carry_w]
    for power_idx in range(3):
        carried.append(
            jnp.einsum("lij,lj->li", kernel, carried[-1], precision=lax.Precision.HIGHEST)
        )
    last_rows = jnp.stack([powers[0][:, -1, :], powers[1][:, -1, :], powers[2][:, -1, :]], 1)
    full_power = powers[3]
    blocks = jnp.moveaxis(values.reshape(full_shape[:-1] + (block_count, block_len)), -2, 0)

    def advance(states, current):
        lasts = jnp.einsum("blrj,lkj->blrk", current, last_rows, precision=lax.Precision.HIGHEST)
        output = jnp.einsum("blrj,lij->blri", current, full_power, precision=lax.Precision.HIGHEST)
        for section_idx in range(4):
            output = (
                output + states[section_idx][..., None] * carried[3 - section_idx][None, :, None, :]
            )
        finals = []
        for section_idx in range(3):
            entry = lasts[..., section_idx]
            for source_idx in range(section_idx + 1):
                entry = (
                    entry
                    + states[source_idx] * carried[section_idx - source_idx][None, :, None, -1]
                )
            finals.append(entry)
        finals.append(output[..., -1])
        return (tuple(finals), output)

    zero_state = tuple((jnp.zeros(full_shape[:-1], jnp.float32) for section_idx in range(4)))
    unused, filtered = lax.scan(advance, zero_state, blocks)
    filtered = jnp.moveaxis(filtered, 0, -2).reshape(full_shape)
    if reverse:
        filtered = jnp.flip(filtered, -1)
    return filtered


def smooth(values, length_scale):
    return recurse(recurse(values, length_scale, False), length_scale, True)


def row_index(lengths, rows_max, row_total):
    starts = jnp.cumsum(lengths) - lengths
    compact = jnp.arange(row_total, dtype=jnp.int32)
    owners = jnp.sum((starts[None, :] <= compact[:, None]).astype(jnp.int32), axis=1) - 1
    chosen = (owners[:, None] == jnp.arange(lengths.shape[0], dtype=jnp.int32)[None, :]).astype(
        jnp.int32
    )
    first_row = jnp.sum(chosen * starts[None, :], axis=1)
    return owners * rows_max + compact - first_row


def body(static_control, alpha_field, perturbations, static_scale, length_x, length_y, lengths):
    rows_max = static_control.shape[2]
    sub_count = lax.axis_size("sub")
    positions = row_index(lengths, rows_max, ROWS_DEV * sub_count)
    here = lax.axis_index("sub")
    own_rows = jnp.sum(jnp.where(jnp.arange(sub_count, dtype=jnp.int32) == here, lengths, 0))
    row_valid = (jnp.arange(rows_max, dtype=jnp.int32) < own_rows).astype(jnp.float32)[
        None, None, :, None
    ]
    factor = jnp.sqrt(length_x * length_y)[None, :, None, None]

    def column_filter(pencils):
        gathered = jnp.take(pencils, positions, axis=2)
        along_y = jnp.moveaxis(smooth(jnp.moveaxis(gathered, 2, 3), length_y), 3, 2)
        return jnp.zeros(pencils.shape, jnp.float32).at[:, :, positions, :].set(along_y * factor)

    vars_here = static_control.shape[0]
    static_x = smooth(static_control * row_valid, length_x)
    static_done = lax.all_to_all(
        column_filter(lax.all_to_all(static_x, "sub", split_axis=3, concat_axis=2, tiled=True)),
        "sub",
        split_axis=2,
        concat_axis=3,
        tiled=True,
    )
    member_x = smooth(alpha_field * row_valid, length_x)
    member_done = lax.all_to_all(
        column_filter(lax.all_to_all(member_x, "sub", split_axis=3, concat_axis=2, tiled=True)),
        "sub",
        split_axis=2,
        concat_axis=3,
        tiled=True,
    )
    partial_sum = perturbations[0].astype(jnp.float32) * member_done[0][None]
    member_count = alpha_field.shape[0] * lax.axis_size("mem")
    summed = lax.psum(partial_sum, "mem")
    own_sum = lax.dynamic_slice_in_dim(summed, lax.axis_index("mem") * vars_here, vars_here, 0)
    return static_scale[:, :, None, None] * static_done + own_sum * (1.0 / math.sqrt(member_count))


MESH = pl.DeviceIdType.MESH
BLK = 128


def response(lag, inverse):
    decay = jnp.exp(-inverse)
    gain = (1.0 - decay) * (1.0 - decay)
    gain = gain * gain * (1.0 / 6.0)
    poly = (lag + 1.0) * (lag + 2.0) * (lag + 3.0)
    value = gain * poly * jnp.exp(-jnp.maximum(lag, 0.0) * inverse)
    return jnp.where(lag >= 0.0, value, 0.0)


def split(values):
    high = values.astype(jnp.bfloat16)
    low = (values - high.astype(jnp.float32)).astype(jnp.bfloat16)
    return high, low


def banded(blocks, weights):
    rows = 8 * len(blocks)
    high, low = split(jnp.concatenate(blocks, axis=0))
    both = jnp.concatenate([high, low], axis=0)
    prod = jnp.dot(both, weights, preferred_element_type=jnp.float32)
    total = prod[:rows, :BLK] + (prod[:rows, BLK:] + prod[rows:, :BLK])
    return [total[8 * b : 8 * b + 8] for b in range(len(blocks))]


def smooth_x(row_values, ahead, back):
    count = row_values.shape[1] // BLK
    zero = jnp.zeros((8, BLK), jnp.float32)
    cells = [zero] + [row_values[:, b * BLK : (b + 1) * BLK] for b in range(count)]
    cells = banded([jnp.concatenate(cells[b : b + 2], axis=1) for b in range(count)], ahead) + [zero]
    return banded([jnp.concatenate(cells[b : b + 2], axis=1) for b in range(count)], back)


def kernel(
    subs, levels, static_ref, alpha_ref, pert_ref, scale_ref, lx_ref, ly_ref, len_ref, out_ref,
    ahead, back, outgo, income, result, done, part, fold, give, take,
    send1, recv1, send2, recv2, send3, recv3, send4, recv4,
):
    me = lax.axis_index("sub")
    mem = lax.axis_index("mem")
    side = lax.rem(mem, 2)
    near = mem + 1 - 2 * side
    far = lax.rem(mem + 2, 4)
    pieces = subs // levels
    width = static_ref.shape[2] // pieces
    per_piece = width // BLK

    barrier = pltpu.get_barrier_semaphore()
    for step in range(1, subs):
        pl.semaphore_signal(
            barrier, inc=1, device_id=(lax.rem(me + step, subs), mem), device_id_type=MESH
        )
    for other in (near, far):
        pl.semaphore_signal(barrier, inc=1, device_id=(me, other), device_id_type=MESH)

    at_in = lax.broadcasted_iota(jnp.int32, (2 * BLK, BLK), 0)
    at_out = lax.broadcasted_iota(jnp.int32, (2 * BLK, BLK), 1)
    lag_ahead = (at_out + BLK - at_in).astype(jnp.float32)
    lag_back = (at_in - at_out).astype(jnp.float32)
    for level in range(levels):
        inverse = 1.0 / jnp.full((1, BLK), lx_ref[level], jnp.float32)
        for ref, lag in ((ahead, lag_ahead), (back, lag_back)):
            high, low = split(response(lag, inverse))
            ref[level, :, :BLK] = high
            ref[level, :, BLK:] = low

    slot = lax.broadcasted_iota(jnp.int32, (8, static_ref.shape[2]), 0)
    valid = slot < len_ref[me]

    def exchange(src, dst, sends, recvs, field, step):
        other = lax.rem(me + step, subs)
        return pltpu.make_async_remote_copy(
            src_ref=src.at[field, other],
            dst_ref=dst.at[field, me],
            send_sem=sends.at[field, step],
            recv_sem=recvs.at[field, me],
            device_id=(other, mem),
            device_id_type=MESH,
        )

    def arrival(src, dst, sends, recvs, field, step):
        other = lax.rem(me + step, subs)
        return pltpu.make_async_remote_copy(
            src_ref=src.at[field, other],
            dst_ref=dst.at[field, other],
            send_sem=sends.at[field, step],
            recv_sem=recvs.at[field, other],
            device_id=(other, mem),
            device_id_type=MESH,
        )

    for field, ref in ((0, alpha_ref), (1, static_ref)):
        for level in range(levels):
            cells = smooth_x(jnp.where(valid, ref[level], 0.0), ahead[level], back[level])
            for piece in range(pieces):
                outgo[field, level * pieces + piece] = jnp.concatenate(
                    cells[piece * per_piece : (piece + 1) * per_piece], axis=1
                )
        if field == 0:
            pl.semaphore_wait(barrier, subs + 1)
        for step in range(1, subs):
            exchange(outgo, income, send1, recv1, field, step).start()
        income[field, me] = outgo[field, me]

    slots = subs * 8
    row = lax.broadcasted_iota(jnp.int32, (slots, slots), 0)
    col = lax.broadcasted_iota(jnp.int32, (slots, slots), 1)
    row_owner, col_owner = row // 8, col // 8
    row_at, col_at = row - 8 * row_owner, col - 8 * col_owner
    row_pos, col_pos, row_len, col_len = row_at, col_at, row * 0, col * 0
    start = 0
    for owner in range(subs):
        held = len_ref[owner]
        row_pos = row_pos + jnp.where(row_owner == owner, start, 0)
        col_pos = col_pos + jnp.where(col_owner == owner, start, 0)
        row_len = row_len + jnp.where(row_owner == owner, held, 0)
        col_len = col_len + jnp.where(col_owner == owner, held, 0)
        start = start + held
    real = jnp.logical_and(row_at < row_len, col_at < col_len)
    lag = (row_pos - col_pos).astype(jnp.float32)
    mine = me // pieces
    len_x = jnp.full((1, slots), lx_ref[mine], jnp.float32)
    len_y = jnp.full((1, slots), ly_ref[mine], jnp.float32)
    inverse = 1.0 / len_y
    lower = jnp.where(real, response(lag, inverse), 0.0)
    upper = jnp.where(real, response(-lag, inverse), 0.0)
    mixed = jnp.dot(
        upper, lower, precision=lax.Precision.HIGHEST, preferred_element_type=jnp.float32
    ) * jnp.sqrt(len_x * len_y)
    mix_high, mix_low = split(mixed)

    for field in range(2):
        for step in range(1, subs):
            arrival(outgo, income, send1, recv1, field, step).wait_recv()
        high, low = split(income[field].reshape(slots, width))
        mixed_rows = jnp.dot(mix_high, high, preferred_element_type=jnp.float32) + (
            jnp.dot(mix_low, high, preferred_element_type=jnp.float32)
            + jnp.dot(mix_high, low, preferred_element_type=jnp.float32)
        )
        result[field] = mixed_rows.reshape(subs, 8, width)
        for step in range(1, subs):
            exchange(result, done, send2, recv2, field, step).start()
        done[field, me] = result[field, me]

    for step in range(1, subs):
        arrival(result, done, send2, recv2, 0, step).wait_recv()

    def weight_rows():
        return [
            jnp.concatenate([done[0, level * pieces + piece] for piece in range(pieces)], axis=1)
            for level in range(levels)
        ]

    weights = jnp.concatenate(weight_rows(), axis=0)
    for half in range(2):
        variable = 2 * half + 1 - side
        part[half] = pert_ref[variable].astype(jnp.float32) * weights
    to_near = pltpu.make_async_remote_copy(
        src_ref=part, dst_ref=fold, send_sem=send3.at[0], recv_sem=recv3.at[0],
        device_id=(me, near), device_id_type=MESH,
    )
    to_near.start()
    top = mem // 2
    own = pert_ref[2 * top + side].astype(jnp.float32) * weights
    passed = pert_ref[2 * (1 - top) + side].astype(jnp.float32) * weights
    to_near.wait_recv()
    give[...] = passed + fold[1 - top]
    to_far = pltpu.make_async_remote_copy(
        src_ref=give, dst_ref=take, send_sem=send4.at[0], recv_sem=recv4.at[0],
        device_id=(me, far), device_id_type=MESH,
    )
    to_far.start()
    own = own + fold[top]
    for step in range(1, subs):
        arrival(result, done, send2, recv2, 1, step).wait_recv()
    to_far.wait_recv()
    total = (own + take[...]) * 0.5
    for level in range(levels):
        fixed = jnp.concatenate(
            [done[1, level * pieces + piece] for piece in range(pieces)], axis=1
        )
        out_ref[level] = scale_ref[0, level] * fixed + total[8 * level : 8 * level + 8]
    for field in range(2):
        for step in range(1, subs):
            exchange(outgo, income, send1, recv1, field, step).wait_send()
            exchange(result, done, send2, recv2, field, step).wait_send()
    to_near.wait_send()
    to_far.wait_send()


def fused(static_control, alpha_field, perturbations, static_scale, length_x, length_y, lengths):
    subs = lax.axis_size("sub")
    unused, levels, rows, cells = static_control.shape
    variables = perturbations.shape[1]
    width = cells // (subs // levels)
    vmem = pl.BlockSpec(memory_space=pltpu.VMEM)
    smem = pl.BlockSpec(memory_space=pltpu.SMEM)
    swap = pltpu.VMEM((2, subs, rows, width), jnp.float32)
    flat = (levels * rows, cells)
    out = pl.pallas_call(
        functools.partial(kernel, subs, levels),
        out_shape=jax.ShapeDtypeStruct((levels, rows, cells), jnp.float32),
        in_specs=[vmem] * 3 + [smem] * 4,
        out_specs=vmem,
        scratch_shapes=[
            pltpu.VMEM((levels, 2 * BLK, 2 * BLK), jnp.bfloat16),
            pltpu.VMEM((levels, 2 * BLK, 2 * BLK), jnp.bfloat16),
            swap, swap, swap, swap,
            pltpu.VMEM((2,) + flat, jnp.float32),
            pltpu.VMEM((2,) + flat, jnp.float32),
            pltpu.VMEM(flat, jnp.float32),
            pltpu.VMEM(flat, jnp.float32),
        ]
        + [pltpu.SemaphoreType.DMA((2, subs))] * 4
        + [pltpu.SemaphoreType.DMA((1,))] * 4,
        compiler_params=pltpu.CompilerParams(
            collective_id=0, has_side_effects=True, vmem_limit_bytes=32 * 1024 * 1024
        ),
    )(
        static_control[0], alpha_field[0], perturbations.reshape((variables,) + flat),
        static_scale, length_x, length_y, lengths,
    )
    return out[None]


def fits(mesh):
    return mesh.shape["sub"] == 8 and mesh.shape["mem"] == 4


def solution(mesh):
    return jax.shard_map(
        fused if fits(mesh) else body,
        mesh=mesh,
        in_specs=(
            P("mem", None, "sub", None),
            P("mem", None, "sub", None),
            P("mem", None, None, "sub", None),
            P("mem", None),
            P(),
            P(),
            P(),
        ),
        out_specs=P("mem", None, "sub", None),
        check_vma=False,
    )
```

```python
import functools
import math

import jax
import jax.numpy as jnp
from jax import lax
from jax.experimental import pallas as pl
from jax.experimental.pallas import tpu as pltpu
from jax.sharding import PartitionSpec as P

ROWS_DEV = 6


def recurse(values, length_scale, reverse):
    full_shape = values.shape
    line_len = full_shape[-1]
    block_len = 128 if line_len % 128 == 0 else line_len
    block_count = line_len // block_len
    if reverse:
        values = jnp.flip(values, -1)
    offsets = jnp.arange(block_len, dtype=jnp.float32)
    lagged = offsets[:, None] - offsets[None, :]
    inverse = 1.0 / length_scale
    decays = jnp.exp(-inverse)
    kernel = jnp.where(
        lagged[None] >= 0.0,
        (1.0 - decays)[:, None, None]
        * jnp.exp(-jnp.maximum(lagged, 0.0)[None] * inverse[:, None, None]),
        0.0,
    )
    carry_w = jnp.exp(-(offsets[None, :] + 1.0) * inverse[:, None])
    powers = [kernel]
    for power_idx in range(3):
        powers.append(
            jnp.einsum("lij,ljk->lik", powers[-1], kernel, precision=lax.Precision.HIGHEST)
        )
    carried = [carry_w]
    for power_idx in range(3):
        carried.append(
            jnp.einsum("lij,lj->li", kernel, carried[-1], precision=lax.Precision.HIGHEST)
        )
    last_rows = jnp.stack([powers[0][:, -1, :], powers[1][:, -1, :], powers[2][:, -1, :]], 1)
    full_power = powers[3]
    blocks = jnp.moveaxis(values.reshape(full_shape[:-1] + (block_count, block_len)), -2, 0)

    def advance(states, current):
        lasts = jnp.einsum("blrj,lkj->blrk", current, last_rows, precision=lax.Precision.HIGHEST)
        output = jnp.einsum("blrj,lij->blri", current, full_power, precision=lax.Precision.HIGHEST)
        for section_idx in range(4):
            output = (
                output + states[section_idx][..., None] * carried[3 - section_idx][None, :, None, :]
            )
        finals = []
        for section_idx in range(3):
            entry = lasts[..., section_idx]
            for source_idx in range(section_idx + 1):
                entry = (
                    entry
                    + states[source_idx] * carried[section_idx - source_idx][None, :, None, -1]
                )
            finals.append(entry)
        finals.append(output[..., -1])
        return (tuple(finals), output)

    zero_state = tuple((jnp.zeros(full_shape[:-1], jnp.float32) for section_idx in range(4)))
    unused, filtered = lax.scan(advance, zero_state, blocks)
    filtered = jnp.moveaxis(filtered, 0, -2).reshape(full_shape)
    if reverse:
        filtered = jnp.flip(filtered, -1)
    return filtered


def smooth(values, length_scale):
    return recurse(recurse(values, length_scale, False), length_scale, True)


def row_index(lengths, rows_max, row_total):
    starts = jnp.cumsum(lengths) - lengths
    compact = jnp.arange(row_total, dtype=jnp.int32)
    owners = jnp.sum((starts[None, :] <= compact[:, None]).astype(jnp.int32), axis=1) - 1
    chosen = (owners[:, None] == jnp.arange(lengths.shape[0], dtype=jnp.int32)[None, :]).astype(
        jnp.int32
    )
    first_row = jnp.sum(chosen * starts[None, :], axis=1)
    return owners * rows_max + compact - first_row


def body(static_control, alpha_field, perturbations, static_scale, length_x, length_y, lengths):
    rows_max = static_control.shape[2]
    sub_count = lax.axis_size("sub")
    positions = row_index(lengths, rows_max, ROWS_DEV * sub_count)
    here = lax.axis_index("sub")
    own_rows = jnp.sum(jnp.where(jnp.arange(sub_count, dtype=jnp.int32) == here, lengths, 0))
    row_valid = (jnp.arange(rows_max, dtype=jnp.int32) < own_rows).astype(jnp.float32)[
        None, None, :, None
    ]
    factor = jnp.sqrt(length_x * length_y)[None, :, None, None]

    def column_filter(pencils):
        gathered = jnp.take(pencils, positions, axis=2)
        along_y = jnp.moveaxis(smooth(jnp.moveaxis(gathered, 2, 3), length_y), 3, 2)
        return jnp.zeros(pencils.shape, jnp.float32).at[:, :, positions, :].set(along_y * factor)

    vars_here = static_control.shape[0]
    static_x = smooth(static_control * row_valid, length_x)
    static_done = lax.all_to_all(
        column_filter(lax.all_to_all(static_x, "sub", split_axis=3, concat_axis=2, tiled=True)),
        "sub",
        split_axis=2,
        concat_axis=3,
        tiled=True,
    )
    member_x = smooth(alpha_field * row_valid, length_x)
    member_done = lax.all_to_all(
        column_filter(lax.all_to_all(member_x, "sub", split_axis=3, concat_axis=2, tiled=True)),
        "sub",
        split_axis=2,
        concat_axis=3,
        tiled=True,
    )
    partial_sum = perturbations[0].astype(jnp.float32) * member_done[0][None]
    member_count = alpha_field.shape[0] * lax.axis_size("mem")
    summed = lax.psum(partial_sum, "mem")
    own_sum = lax.dynamic_slice_in_dim(summed, lax.axis_index("mem") * vars_here, vars_here, 0)
    return static_scale[:, :, None, None] * static_done + own_sum * (1.0 / math.sqrt(member_count))


MESH = pl.DeviceIdType.MESH
BLK = 128
HIGHEST = lax.Precision.HIGHEST


def taps(lag, depth, inverse):
    rest = 1.0 - jnp.exp(-inverse)
    value = jnp.exp(-jnp.maximum(lag, 0.0) * inverse)
    for order in range(1, 4):
        factor = rest * (lag + float(order)) * (1.0 / order)
        if isinstance(depth, int):
            value = value * factor if depth >= order else value
        else:
            value = value * jnp.where(depth >= order, factor, 1.0)
    return jnp.where(lag >= 0.0, value, 0.0)


def passed(lag, depth, inverse):
    return taps(lag, depth, inverse) * (1.0 - jnp.exp(-inverse))


def split(values):
    high = values.astype(jnp.bfloat16)
    low = (values - high.astype(jnp.float32)).astype(jnp.bfloat16)
    return high, low


def product(matrix, values):
    mat_high, mat_low = matrix
    high, low = split(values)
    return jnp.dot(mat_high, high, preferred_element_type=jnp.float32) + (
        jnp.dot(mat_low, high, preferred_element_type=jnp.float32)
        + jnp.dot(mat_high, low, preferred_element_type=jnp.float32)
    )


def banded(blocks, weights):
    rows = 8 * len(blocks)
    high, low = split(jnp.concatenate(blocks, axis=0))
    both = jnp.concatenate([high, low], axis=0)
    prod = jnp.dot(both, weights, preferred_element_type=jnp.float32)
    total = prod[:rows, :BLK] + (prod[:rows, BLK:] + prod[rows:, :BLK])
    return [total[8 * b : 8 * b + 8] for b in range(len(blocks))]


def smooth_x(row_values, ahead, back):
    count = row_values.shape[1] // BLK
    zero = jnp.zeros((8, BLK), jnp.float32)
    cells = [zero] + [row_values[:, b * BLK : (b + 1) * BLK] for b in range(count)]
    cells = banded([jnp.concatenate(cells[b : b + 2], axis=1) for b in range(count)], ahead) + [zero]
    return banded([jnp.concatenate(cells[b : b + 2], axis=1) for b in range(count)], back)


def choose(index, options):
    value = options[0]
    for which in range(1, len(options)):
        value = jnp.where(index == which, options[which], value)
    return value


def line_matrices(group, groups, levels, lx_ref, ly_ref, len_ref):
    subs = 2 * groups
    held = [len_ref[sub] for sub in range(subs)]
    starts = [jnp.int32(0)]
    for sub in range(subs):
        starts.append(starts[-1] + held[sub])
    edges = [starts[2 * g] for g in range(groups + 1)]

    def iota(shape, axis):
        return lax.broadcasted_iota(jnp.int32, shape, axis)

    def own_slots(index):
        sub = 2 * group + index // 32
        slot = index % 8
        where = choose(sub, starts[:subs]) + slot
        real = slot < choose(sub, held)
        return where.astype(jnp.float32), real, (index // 8) % 4

    def scale_of(level, ref):
        return choose(level, [ref[lev] for lev in range(levels)])

    rows = 16 * levels
    slots = 8 * subs
    far_cols = (groups - 1) * 4 * levels
    row_at, row_real, row_level = own_slots(iota((rows, 1), 0))
    col_at, col_real, col_level = own_slots(iota((1, rows), 1))
    row_len = scale_of(row_level, ly_ref) + jnp.zeros((rows, 1), jnp.float32)
    row_inv = 1.0 / row_len
    col_inv = 1.0 / (scale_of(col_level, ly_ref) + jnp.zeros((1, rows), jnp.float32))

    def all_slots(index):
        sub, slot = index // 8, index % 8
        where = choose(sub, starts[:subs]) + slot
        return where.astype(jnp.float32), slot < choose(sub, held)

    k_col_at, k_col_real = all_slots(iota((slots, 1), 0))
    k_row_at, k_row_real = all_slots(iota((1, slots), 1))

    far = iota((1, far_cols), 1)
    far_step = far // (4 * levels) + 1
    far_level = (far // 4) % levels
    far_state = far % 4
    far_group = far_step * -1 + group
    far_group = jnp.where(far_group < 0, far_group + groups, far_group)
    far_inv = 1.0 / (scale_of(far_level, ly_ref) + jnp.zeros((1, far_cols), jnp.float32))
    far_before = far_group < group
    far_first = choose(far_group, edges[:groups]).astype(jnp.float32)
    far_end = choose(far_group, edges[1:]).astype(jnp.float32)
    far_depth = 3 - far_state
    far_decay = jnp.exp(-far_inv)

    forward = jnp.where(
        jnp.logical_and(k_col_real, col_real), passed(k_col_at - col_at, 3, col_inv), 0.0
    )
    entry = jnp.where(
        k_col_real, taps(k_col_at - far_end, far_depth, far_inv) * far_decay, 0.0
    )
    backward = jnp.where(
        jnp.logical_and(row_real, k_row_real), passed(k_row_at - row_at, 3, row_inv), 0.0
    )
    inner = jnp.dot(backward, forward, precision=HIGHEST, preferred_element_type=jnp.float32)
    outer = jnp.dot(backward, entry, precision=HIGHEST, preferred_element_type=jnp.float32)
    behind = jnp.where(
        row_real, taps(far_first - 1.0 - row_at, far_depth, far_inv) * far_decay, 0.0
    )
    outer = jnp.where(far_before, outer, behind)
    factor = jnp.sqrt(scale_of(row_level, lx_ref) * row_len)
    inner = jnp.where(row_level == col_level, inner, 0.0) * factor
    outer = jnp.where(row_level == far_level, outer, 0.0) * factor

    state_rows = 4 * levels
    st = iota((state_rows, 1), 0)
    st_level, st_depth = st // 4, st % 4
    st_inv = 1.0 / (scale_of(st_level, ly_ref) + jnp.zeros((state_rows, 1), jnp.float32))
    first = choose(group, edges[:groups]).astype(jnp.float32)
    end = choose(group, edges[1:]).astype(jnp.float32)
    leaving = jnp.where(col_real, passed(end - 1.0 - col_at, st_depth, st_inv), 0.0)
    turned = jnp.where(k_row_real, passed(k_row_at - first, st_depth, st_inv), 0.0)
    turned = jnp.dot(turned, forward, precision=HIGHEST, preferred_element_type=jnp.float32)
    moments = [
        jnp.where(st_level == col_level, part, 0.0) for part in (leaving, turned)
    ]
    return jnp.concatenate(moments, axis=0), inner, outer


def kernel(
    groups, levels, static_hbm, alpha_hbm, pert_hbm, scale_ref, lx_ref, ly_ref, len_ref, out_ref,
    static_ref, alpha_ref, pert_ref, ahead, back, outgo, pair, mom, msg, result, done,
    part, fold, give, take, own,
    load, send1, recv1, send2, recv2, send3, recv3, send4, recv4, send5, recv5,
):
    me = lax.axis_index("sub")
    mem = lax.axis_index("mem")
    group, side = me // 2, lax.rem(me, 2)
    beside = me + 1 - 2 * side
    core = lax.rem(mem, 2)
    near = mem + 1 - 2 * core
    far = lax.rem(mem + 2, 4)
    top = mem // 2
    state_rows = 4 * levels
    half_rows = 8 * levels
    width = static_ref.shape[2] // 2
    per_half = width // BLK

    loads = [
        pltpu.make_async_copy(src, dst, load.at[which])
        for which, (src, dst) in enumerate(
            ((alpha_hbm, alpha_ref), (static_hbm, static_ref), (pert_hbm, pert_ref))
        )
    ]
    for one in loads:
        one.start()

    barrier = pltpu.get_barrier_semaphore()
    friends = [(beside, mem), (me, near), (me, far)]
    for step in range(1, groups):
        friends.append((2 * lax.rem(group + step, groups) + side, mem))
    for friend in friends:
        pl.semaphore_signal(barrier, inc=1, device_id=friend, device_id_type=MESH)

    at_in = lax.broadcasted_iota(jnp.int32, (2 * BLK, BLK), 0)
    at_out = lax.broadcasted_iota(jnp.int32, (2 * BLK, BLK), 1)
    lag_ahead = (at_out + BLK - at_in).astype(jnp.float32)
    lag_back = (at_in - at_out).astype(jnp.float32)
    for level in range(levels):
        inverse = 1.0 / jnp.full((1, BLK), lx_ref[level], jnp.float32)
        for ref, lag in ((ahead, lag_ahead), (back, lag_back)):
            high, low = split(passed(lag, 3, inverse))
            ref[level, :, :BLK] = high
            ref[level, :, BLK:] = low

    slot = lax.broadcasted_iota(jnp.int32, (8, static_ref.shape[2]), 0)
    valid = slot < len_ref[me]

    def to_pair(field):
        return pltpu.make_async_remote_copy(
            src_ref=outgo.at[field, 1 - side], dst_ref=pair.at[field, side],
            send_sem=send1.at[field], recv_sem=recv1.at[field],
            device_id=(beside, mem), device_id_type=MESH,
        )

    def from_pair(field):
        return pltpu.make_async_remote_copy(
            src_ref=outgo.at[field, 1 - side], dst_ref=pair.at[field, 1 - side],
            send_sem=send1.at[field], recv_sem=recv1.at[field],
            device_id=(beside, mem), device_id_type=MESH,
        )

    def to_group(field, step):
        other = lax.rem(group + step, groups)
        kind = jnp.where(other > group, 0, 1)
        return pltpu.make_async_remote_copy(
            src_ref=mom.at[field, kind], dst_ref=msg.at[field, step - 1],
            send_sem=send2.at[field, step], recv_sem=recv2.at[field, step],
            device_id=(2 * other + side, mem), device_id_type=MESH,
        )

    def to_home(field):
        return pltpu.make_async_remote_copy(
            src_ref=result.at[field], dst_ref=done.at[field, side],
            send_sem=send3.at[field], recv_sem=recv3.at[field],
            device_id=(beside, mem), device_id_type=MESH,
        )

    def from_home(field):
        return pltpu.make_async_remote_copy(
            src_ref=result.at[field], dst_ref=done.at[field, 1 - side],
            send_sem=send3.at[field], recv_sem=recv3.at[field],
            device_id=(beside, mem), device_id_type=MESH,
        )

    def to_near(half):
        return pltpu.make_async_remote_copy(
            src_ref=part.at[half], dst_ref=fold.at[half],
            send_sem=send4.at[half], recv_sem=recv4.at[half],
            device_id=(me, near), device_id_type=MESH,
        )

    def to_far(half):
        return pltpu.make_async_remote_copy(
            src_ref=give.at[half], dst_ref=take.at[half],
            send_sem=send5.at[half], recv_sem=recv5.at[half],
            device_id=(me, far), device_id_type=MESH,
        )

    for field, ref in ((0, alpha_ref), (1, static_ref)):
        loads[field].wait()
        for level in range(levels):
            cells = smooth_x(jnp.where(valid, ref[level], 0.0), ahead[level], back[level])
            for half in range(2):
                outgo[field, half, 8 * level : 8 * level + 8] = jnp.concatenate(
                    cells[half * per_half : (half + 1) * per_half], axis=1
                )
        if field == 0:
            pl.semaphore_wait(barrier, len(friends))
        to_pair(field).start()
        pair[field, side] = outgo[field, side]

    moments, inner, outer = line_matrices(group, groups, levels, lx_ref, ly_ref, len_ref)
    moments, inner, outer = split(moments), split(inner), split(outer)

    def pair_rows(field):
        return jnp.concatenate([pair[field, 0], pair[field, 1]], axis=0)

    for field in range(2):
        from_pair(field).wait_recv()
        both = product(moments, pair_rows(field))
        for kind in range(2):
            mom[field, kind] = both[kind * state_rows : (kind + 1) * state_rows]
        for step in range(1, groups):
            to_group(field, step).start()

    def finish(field):
        mixed = product(inner, pair_rows(field))
        for step in range(1, groups):
            to_group(field, step).wait_recv()
        arrived = jnp.concatenate([msg[field, step] for step in range(groups - 1)], axis=0)
        mixed = mixed + product(outer, arrived)
        mine, theirs = mixed[:half_rows], mixed[half_rows:]
        result[field] = jnp.where(side == 0, theirs, mine)
        to_home(field).start()
        done[field, side] = jnp.where(side == 0, mine, theirs)

    def terms(half, variable):
        columns = pl.ds(pl.multiple_of(half * width, BLK), width)
        return pert_ref[variable, :, columns].astype(jnp.float32) * done[0, half]

    def gather(half):
        for which in range(2):
            part[half, which] = terms(half, 2 * which + 1 - core)
        to_near(half).start()

    def forward_sum(half):
        to_near(half).wait_recv()
        give[half] = terms(half, 2 * (1 - top) + core) + fold[half, 1 - top]
        to_far(half).start()
        own[half] = terms(half, 2 * top + core) + fold[half, top]

    finish(0)
    loads[2].wait()
    gather(side)
    forward_sum(side)
    from_home(0).wait_recv()
    gather(1 - side)
    forward_sum(1 - side)
    finish(1)

    def write(half):
        to_far(half).wait_recv()
        total = (own[half] + take[half]) * 0.5
        columns = pl.ds(pl.multiple_of(half * width, BLK), width)
        for level in range(levels):
            rows = slice(8 * level, 8 * level + 8)
            out_ref[level, :, columns] = (
                scale_ref[0, level] * done[1, half, rows] + total[rows]
            )

    write(side)
    from_home(1).wait_recv()
    write(1 - side)
    for field in range(2):
        to_pair(field).wait_send()
        to_home(field).wait_send()
        for step in range(1, groups):
            to_group(field, step).wait_send()
    for half in (side, 1 - side):
        to_near(half).wait_send()
        to_far(half).wait_send()


def fused(static_control, alpha_field, perturbations, static_scale, length_x, length_y, lengths):
    groups = lax.axis_size("sub") // 2
    unused, levels, rows, cells = static_control.shape
    variables = perturbations.shape[1]
    width = cells // 2
    flat = (levels * rows, width)
    anywhere = pl.BlockSpec(memory_space=pl.ANY)
    smem = pl.BlockSpec(memory_space=pltpu.SMEM)

    def buffer(*shape):
        return pltpu.VMEM(shape, jnp.float32)

    dma = pltpu.SemaphoreType.DMA
    out = pl.pallas_call(
        functools.partial(kernel, groups, levels),
        out_shape=jax.ShapeDtypeStruct((levels, rows, cells), jnp.float32),
        in_specs=[anywhere] * 3 + [smem] * 4,
        out_specs=pl.BlockSpec(memory_space=pltpu.VMEM),
        scratch_shapes=[
            buffer(levels, rows, cells),
            buffer(levels, rows, cells),
            pltpu.VMEM((variables, levels * rows, cells), jnp.bfloat16),
            pltpu.VMEM((levels, 2 * BLK, 2 * BLK), jnp.bfloat16),
            pltpu.VMEM((levels, 2 * BLK, 2 * BLK), jnp.bfloat16),
            buffer(2, 2, *flat),
            buffer(2, 2, *flat),
            buffer(2, 2, 4 * levels, width),
            buffer(2, groups - 1, 4 * levels, width),
            buffer(2, *flat),
            buffer(2, 2, *flat),
            buffer(2, 2, *flat),
            buffer(2, 2, *flat),
            buffer(2, *flat),
            buffer(2, *flat),
            buffer(2, *flat),
            dma((3,)),
            dma((2,)), dma((2,)),
            dma((2, groups)), dma((2, groups)),
            dma((2,)), dma((2,)),
            dma((2,)), dma((2,)),
            dma((2,)), dma((2,)),
        ],
        compiler_params=pltpu.CompilerParams(
            collective_id=0, has_side_effects=True, vmem_limit_bytes=60 * 1024 * 1024
        ),
    )(
        static_control[0], alpha_field[0],
        perturbations.reshape(variables, levels * rows, cells),
        static_scale, length_x, length_y, lengths,
    )
    return out[None]


def fits(mesh):
    return mesh.shape["sub"] == 8 and mesh.shape["mem"] == 4


def solution(mesh):
    return jax.shard_map(
        fused if fits(mesh) else body,
        mesh=mesh,
        in_specs=(
            P("mem", None, "sub", None),
            P("mem", None, "sub", None),
            P("mem", None, None, "sub", None),
            P("mem", None),
            P(),
            P(),
            P(),
        ),
        out_specs=P("mem", None, "sub", None),
        check_vma=False,
    )
```

```python
import functools
import math

import jax
import jax.numpy as jnp
from jax import lax
from jax.experimental import pallas as pl
from jax.experimental.pallas import tpu as pltpu
from jax.sharding import PartitionSpec as P

ROWS_DEV = 6


def recurse(values, length_scale, reverse):
    full_shape = values.shape
    line_len = full_shape[-1]
    block_len = 128 if line_len % 128 == 0 else line_len
    block_count = line_len // block_len
    if reverse:
        values = jnp.flip(values, -1)
    offsets = jnp.arange(block_len, dtype=jnp.float32)
    lagged = offsets[:, None] - offsets[None, :]
    inverse = 1.0 / length_scale
    decays = jnp.exp(-inverse)
    kernel = jnp.where(
        lagged[None] >= 0.0,
        (1.0 - decays)[:, None, None]
        * jnp.exp(-jnp.maximum(lagged, 0.0)[None] * inverse[:, None, None]),
        0.0,
    )
    carry_w = jnp.exp(-(offsets[None, :] + 1.0) * inverse[:, None])
    powers = [kernel]
    for power_idx in range(3):
        powers.append(
            jnp.einsum("lij,ljk->lik", powers[-1], kernel, precision=lax.Precision.HIGHEST)
        )
    carried = [carry_w]
    for power_idx in range(3):
        carried.append(
            jnp.einsum("lij,lj->li", kernel, carried[-1], precision=lax.Precision.HIGHEST)
        )
    last_rows = jnp.stack([powers[0][:, -1, :], powers[1][:, -1, :], powers[2][:, -1, :]], 1)
    full_power = powers[3]
    blocks = jnp.moveaxis(values.reshape(full_shape[:-1] + (block_count, block_len)), -2, 0)

    def advance(states, current):
        lasts = jnp.einsum("blrj,lkj->blrk", current, last_rows, precision=lax.Precision.HIGHEST)
        output = jnp.einsum("blrj,lij->blri", current, full_power, precision=lax.Precision.HIGHEST)
        for section_idx in range(4):
            output = (
                output + states[section_idx][..., None] * carried[3 - section_idx][None, :, None, :]
            )
        finals = []
        for section_idx in range(3):
            entry = lasts[..., section_idx]
            for source_idx in range(section_idx + 1):
                entry = (
                    entry
                    + states[source_idx] * carried[section_idx - source_idx][None, :, None, -1]
                )
            finals.append(entry)
        finals.append(output[..., -1])
        return (tuple(finals), output)

    zero_state = tuple((jnp.zeros(full_shape[:-1], jnp.float32) for section_idx in range(4)))
    unused, filtered = lax.scan(advance, zero_state, blocks)
    filtered = jnp.moveaxis(filtered, 0, -2).reshape(full_shape)
    if reverse:
        filtered = jnp.flip(filtered, -1)
    return filtered


def smooth(values, length_scale):
    return recurse(recurse(values, length_scale, False), length_scale, True)


def row_index(lengths, rows_max, row_total):
    starts = jnp.cumsum(lengths) - lengths
    compact = jnp.arange(row_total, dtype=jnp.int32)
    owners = jnp.sum((starts[None, :] <= compact[:, None]).astype(jnp.int32), axis=1) - 1
    chosen = (owners[:, None] == jnp.arange(lengths.shape[0], dtype=jnp.int32)[None, :]).astype(
        jnp.int32
    )
    first_row = jnp.sum(chosen * starts[None, :], axis=1)
    return owners * rows_max + compact - first_row


def body(static_control, alpha_field, perturbations, static_scale, length_x, length_y, lengths):
    rows_max = static_control.shape[2]
    sub_count = lax.axis_size("sub")
    positions = row_index(lengths, rows_max, ROWS_DEV * sub_count)
    here = lax.axis_index("sub")
    own_rows = jnp.sum(jnp.where(jnp.arange(sub_count, dtype=jnp.int32) == here, lengths, 0))
    row_valid = (jnp.arange(rows_max, dtype=jnp.int32) < own_rows).astype(jnp.float32)[
        None, None, :, None
    ]
    factor = jnp.sqrt(length_x * length_y)[None, :, None, None]

    def column_filter(pencils):
        gathered = jnp.take(pencils, positions, axis=2)
        along_y = jnp.moveaxis(smooth(jnp.moveaxis(gathered, 2, 3), length_y), 3, 2)
        return jnp.zeros(pencils.shape, jnp.float32).at[:, :, positions, :].set(along_y * factor)

    vars_here = static_control.shape[0]
    static_x = smooth(static_control * row_valid, length_x)
    static_done = lax.all_to_all(
        column_filter(lax.all_to_all(static_x, "sub", split_axis=3, concat_axis=2, tiled=True)),
        "sub",
        split_axis=2,
        concat_axis=3,
        tiled=True,
    )
    member_x = smooth(alpha_field * row_valid, length_x)
    member_done = lax.all_to_all(
        column_filter(lax.all_to_all(member_x, "sub", split_axis=3, concat_axis=2, tiled=True)),
        "sub",
        split_axis=2,
        concat_axis=3,
        tiled=True,
    )
    partial_sum = perturbations[0].astype(jnp.float32) * member_done[0][None]
    member_count = alpha_field.shape[0] * lax.axis_size("mem")
    summed = lax.psum(partial_sum, "mem")
    own_sum = lax.dynamic_slice_in_dim(summed, lax.axis_index("mem") * vars_here, vars_here, 0)
    return static_scale[:, :, None, None] * static_done + own_sum * (1.0 / math.sqrt(member_count))


MESH = pl.DeviceIdType.MESH
PARTS = 2
BLK = 128
HIGHEST = lax.Precision.HIGHEST


def taps(lag, depth, inverse):
    rest = 1.0 - jnp.exp(-inverse)
    value = jnp.exp(-jnp.maximum(lag, 0.0) * inverse)
    for order in range(1, 4):
        factor = rest * (lag + float(order)) * (1.0 / order)
        if isinstance(depth, int):
            value = value * factor if depth >= order else value
        else:
            value = value * jnp.where(depth >= order, factor, 1.0)
    return jnp.where(lag >= 0.0, value, 0.0)


def passed(lag, depth, inverse):
    return taps(lag, depth, inverse) * (1.0 - jnp.exp(-inverse))


def split(values):
    high = values.astype(jnp.bfloat16)
    low = (values - high.astype(jnp.float32)).astype(jnp.bfloat16)
    return high, low


def product(matrix, values):
    mat_high, mat_low = matrix
    high, low = split(values)
    return jnp.dot(mat_high, high, preferred_element_type=jnp.float32) + (
        jnp.dot(mat_low, high, preferred_element_type=jnp.float32)
        + jnp.dot(mat_high, low, preferred_element_type=jnp.float32)
    )


def banded(blocks, weights):
    rows = 8 * len(blocks)
    high, low = split(jnp.concatenate(blocks, axis=0))
    both = jnp.concatenate([high, low], axis=0)
    prod = jnp.dot(both, weights, preferred_element_type=jnp.float32)
    total = prod[:rows, :BLK] + (prod[:rows, BLK:] + prod[rows:, :BLK])
    return [total[8 * b : 8 * b + 8] for b in range(len(blocks))]


def smooth_x(row_values, ahead, back):
    count = row_values.shape[1] // BLK
    zero = jnp.zeros((8, BLK), jnp.float32)
    cells = [zero] + [row_values[:, b * BLK : (b + 1) * BLK] for b in range(count)]
    cells = banded([jnp.concatenate(cells[b : b + 2], axis=1) for b in range(count)], ahead) + [zero]
    return banded([jnp.concatenate(cells[b : b + 2], axis=1) for b in range(count)], back)


def choose(index, options):
    value = options[0]
    for which in range(1, len(options)):
        value = jnp.where(index == which, options[which], value)
    return value


def line_matrices(group, groups, levels, lx_ref, ly_ref, len_ref):
    subs = 2 * groups
    held = [len_ref[sub] for sub in range(subs)]
    starts = [jnp.int32(0)]
    for sub in range(subs):
        starts.append(starts[-1] + held[sub])
    edges = [starts[2 * g] for g in range(groups + 1)]

    def iota(shape, axis):
        return lax.broadcasted_iota(jnp.int32, shape, axis)

    def own_slots(index):
        sub = 2 * group + index // 32
        slot = index % 8
        where = choose(sub, starts[:subs]) + slot
        real = slot < choose(sub, held)
        return where.astype(jnp.float32), real, (index // 8) % 4

    def scale_of(level, ref):
        return choose(level, [ref[lev] for lev in range(levels)])

    rows = 16 * levels
    slots = 8 * subs
    far_cols = (groups - 1) * 4 * levels
    row_at, row_real, row_level = own_slots(iota((rows, 1), 0))
    col_at, col_real, col_level = own_slots(iota((1, rows), 1))
    row_len = scale_of(row_level, ly_ref) + jnp.zeros((rows, 1), jnp.float32)
    row_inv = 1.0 / row_len
    col_inv = 1.0 / (scale_of(col_level, ly_ref) + jnp.zeros((1, rows), jnp.float32))

    def all_slots(index):
        sub, slot = index // 8, index % 8
        where = choose(sub, starts[:subs]) + slot
        return where.astype(jnp.float32), slot < choose(sub, held)

    k_col_at, k_col_real = all_slots(iota((slots, 1), 0))
    k_row_at, k_row_real = all_slots(iota((1, slots), 1))

    far = iota((1, far_cols), 1)
    far_step = far // (4 * levels) + 1
    far_level = (far // 4) % levels
    far_state = far % 4
    far_group = far_step * -1 + group
    far_group = jnp.where(far_group < 0, far_group + groups, far_group)
    far_inv = 1.0 / (scale_of(far_level, ly_ref) + jnp.zeros((1, far_cols), jnp.float32))
    far_before = far_group < group
    far_first = choose(far_group, edges[:groups]).astype(jnp.float32)
    far_end = choose(far_group, edges[1:]).astype(jnp.float32)
    far_depth = 3 - far_state
    far_decay = jnp.exp(-far_inv)

    forward = jnp.where(
        jnp.logical_and(k_col_real, col_real), passed(k_col_at - col_at, 3, col_inv), 0.0
    )
    entry = jnp.where(
        k_col_real, taps(k_col_at - far_end, far_depth, far_inv) * far_decay, 0.0
    )
    backward = jnp.where(
        jnp.logical_and(row_real, k_row_real), passed(k_row_at - row_at, 3, row_inv), 0.0
    )
    inner = jnp.dot(backward, forward, precision=HIGHEST, preferred_element_type=jnp.float32)
    outer = jnp.dot(backward, entry, precision=HIGHEST, preferred_element_type=jnp.float32)
    behind = jnp.where(
        row_real, taps(far_first - 1.0 - row_at, far_depth, far_inv) * far_decay, 0.0
    )
    outer = jnp.where(far_before, outer, behind)
    factor = jnp.sqrt(scale_of(row_level, lx_ref) * row_len)
    inner = jnp.where(row_level == col_level, inner, 0.0) * factor
    outer = jnp.where(row_level == far_level, outer, 0.0) * factor

    state_rows = 4 * levels
    st = iota((state_rows, 1), 0)
    st_level, st_depth = st // 4, st % 4
    st_inv = 1.0 / (scale_of(st_level, ly_ref) + jnp.zeros((state_rows, 1), jnp.float32))
    first = choose(group, edges[:groups]).astype(jnp.float32)
    end = choose(group, edges[1:]).astype(jnp.float32)
    leaving = jnp.where(col_real, passed(end - 1.0 - col_at, st_depth, st_inv), 0.0)
    turned = jnp.where(k_row_real, passed(k_row_at - first, st_depth, st_inv), 0.0)
    turned = jnp.dot(turned, forward, precision=HIGHEST, preferred_element_type=jnp.float32)
    moments = [
        jnp.where(st_level == col_level, part, 0.0) for part in (leaving, turned)
    ]
    return jnp.concatenate(moments, axis=0), inner, outer


def kernel(
    groups, levels, static_hbm, alpha_hbm, pert_hbm, scale_ref, lx_ref, ly_ref, len_ref, out_ref,
    static_ref, alpha_ref, pert_ref, ahead, back, outgo, pair, mom, msg, result, done,
    part, fold, give, take, own,
    load, send1, recv1, send2, recv2, send3, recv3, send4, recv4, send5, recv5,
):
    me = lax.axis_index("sub")
    mem = lax.axis_index("mem")
    group, side = me // 2, lax.rem(me, 2)
    beside = me + 1 - 2 * side
    core = lax.rem(mem, 2)
    near = mem + 1 - 2 * core
    far = lax.rem(mem + 2, 4)
    top = mem // 2
    state_rows = 4 * levels
    half_rows = 8 * levels
    width = static_ref.shape[2] // (2 * PARTS)
    per_part = width // BLK
    units = 2 * PARTS

    loads = [
        pltpu.make_async_copy(src, dst, load.at[which])
        for which, (src, dst) in enumerate(
            ((alpha_hbm, alpha_ref), (static_hbm, static_ref), (pert_hbm, pert_ref))
        )
    ]
    for one in loads:
        one.start()

    barrier = pltpu.get_barrier_semaphore()
    friends = [(beside, mem), (me, near), (me, far)]
    for step in range(1, groups):
        friends.append((2 * lax.rem(group + step, groups) + side, mem))
    for friend in friends:
        pl.semaphore_signal(barrier, inc=1, device_id=friend, device_id_type=MESH)

    at_in = lax.broadcasted_iota(jnp.int32, (2 * BLK, BLK), 0)
    at_out = lax.broadcasted_iota(jnp.int32, (2 * BLK, BLK), 1)
    lag_ahead = (at_out + BLK - at_in).astype(jnp.float32)
    lag_back = (at_in - at_out).astype(jnp.float32)
    for level in range(levels):
        inverse = 1.0 / jnp.full((1, BLK), lx_ref[level], jnp.float32)
        for ref, lag in ((ahead, lag_ahead), (back, lag_back)):
            high, low = split(passed(lag, 3, inverse))
            ref[level, :, :BLK] = high
            ref[level, :, BLK:] = low

    slot = lax.broadcasted_iota(jnp.int32, (8, static_ref.shape[2]), 0)
    valid = slot < len_ref[me]

    def to_pair(field):
        return pltpu.make_async_remote_copy(
            src_ref=outgo.at[field, 1 - side], dst_ref=pair.at[field, side],
            send_sem=send1.at[field], recv_sem=recv1.at[field],
            device_id=(beside, mem), device_id_type=MESH,
        )

    def from_pair(field):
        return pltpu.make_async_remote_copy(
            src_ref=outgo.at[field, 1 - side], dst_ref=pair.at[field, 1 - side],
            send_sem=send1.at[field], recv_sem=recv1.at[field],
            device_id=(beside, mem), device_id_type=MESH,
        )

    def to_group(field, step):
        other = lax.rem(group + step, groups)
        kind = jnp.where(other > group, 0, 1)
        return pltpu.make_async_remote_copy(
            src_ref=mom.at[field, kind], dst_ref=msg.at[field, step - 1],
            send_sem=send2.at[field, step], recv_sem=recv2.at[field, step],
            device_id=(2 * other + side, mem), device_id_type=MESH,
        )

    def to_home(field):
        return pltpu.make_async_remote_copy(
            src_ref=result.at[field], dst_ref=done.at[field, side],
            send_sem=send3.at[field], recv_sem=recv3.at[field],
            device_id=(beside, mem), device_id_type=MESH,
        )

    def from_home(field):
        return pltpu.make_async_remote_copy(
            src_ref=result.at[field], dst_ref=done.at[field, 1 - side],
            send_sem=send3.at[field], recv_sem=recv3.at[field],
            device_id=(beside, mem), device_id_type=MESH,
        )

    def to_near(half, piece):
        return pltpu.make_async_remote_copy(
            src_ref=part.at[half, piece], dst_ref=fold.at[half, piece],
            send_sem=send4.at[half, piece], recv_sem=recv4.at[half, piece],
            device_id=(me, near), device_id_type=MESH,
        )

    def to_far(half, piece):
        return pltpu.make_async_remote_copy(
            src_ref=give.at[half, piece], dst_ref=take.at[half, piece],
            send_sem=send5.at[half, piece], recv_sem=recv5.at[half, piece],
            device_id=(me, far), device_id_type=MESH,
        )

    for field, ref in ((0, alpha_ref), (1, static_ref)):
        loads[field].wait()
        for level in range(levels):
            cells = smooth_x(jnp.where(valid, ref[level], 0.0), ahead[level], back[level])
            for half in range(2):
                for piece in range(PARTS):
                    first = (half * PARTS + piece) * per_part
                    outgo[field * PARTS + piece, half, 8 * level : 8 * level + 8] = jnp.concatenate(
                        cells[first : first + per_part], axis=1
                    )
        if field == 0:
            pl.semaphore_wait(barrier, len(friends))
        for unit in range(field * PARTS, (field + 1) * PARTS):
            to_pair(unit).start()
        for unit in range(field * PARTS, (field + 1) * PARTS):
            pair[unit, side] = outgo[unit, side]

    moments, inner, outer = line_matrices(group, groups, levels, lx_ref, ly_ref, len_ref)
    moments, inner, outer = split(moments), split(inner), split(outer)

    def pair_rows(field):
        return jnp.concatenate([pair[field, 0], pair[field, 1]], axis=0)

    def spread(field):
        from_pair(field).wait_recv()
        both = product(moments, pair_rows(field))
        for kind in range(2):
            mom[field, kind] = both[kind * state_rows : (kind + 1) * state_rows]
        for step in range(1, groups):
            to_group(field, step).start()

    for piece in range(PARTS):
        spread(piece)

    def finish(field):
        mixed = product(inner, pair_rows(field))
        for step in range(1, groups):
            to_group(field, step).wait_recv()
        arrived = jnp.concatenate([msg[field, step] for step in range(groups - 1)], axis=0)
        mixed = mixed + product(outer, arrived)
        mine, theirs = mixed[:half_rows], mixed[half_rows:]
        result[field] = jnp.where(side == 0, theirs, mine)
        to_home(field).start()
        done[field, side] = jnp.where(side == 0, mine, theirs)

    def columns(half, piece):
        return pl.ds(pl.multiple_of((half * PARTS + piece) * width, BLK), width)

    def terms(half, piece, variable):
        return pert_ref[variable, :, columns(half, piece)].astype(jnp.float32) * done[piece, half]

    def gather(half, piece):
        for which in range(2):
            part[half, piece, which] = terms(half, piece, 2 * which + 1 - core)
        to_near(half, piece).start()

    def forward_sum(half, piece):
        to_near(half, piece).wait_recv()
        give[half, piece] = (
            terms(half, piece, 2 * (1 - top) + core) + fold[half, piece, 1 - top]
        )
        to_far(half, piece).start()
        own[half, piece] = terms(half, piece, 2 * top + core) + fold[half, piece, top]

    def write(half, piece):
        to_far(half, piece).wait_recv()
        total = (own[half, piece] + take[half, piece]) * 0.5
        for level in range(levels):
            rows = slice(8 * level, 8 * level + 8)
            out_ref[level, :, columns(half, piece)] = (
                scale_ref[0, level] * done[PARTS + piece, half, rows] + total[rows]
            )

    pieces = range(PARTS)
    for piece in pieces:
        finish(piece)
        if piece == 0:
            loads[2].wait()
        gather(side, piece)
        spread(PARTS + piece)
    for piece in pieces:
        forward_sum(side, piece)
        from_home(piece).wait_recv()
        gather(1 - side, piece)
    finish(PARTS)
    for piece in pieces:
        forward_sum(1 - side, piece)
    for piece in range(1, PARTS):
        finish(PARTS + piece)
    for piece in pieces:
        write(side, piece)
    for piece in pieces:
        from_home(PARTS + piece).wait_recv()
        write(1 - side, piece)
    for field in range(units):
        to_pair(field).wait_send()
        to_home(field).wait_send()
        for step in range(1, groups):
            to_group(field, step).wait_send()
    for half in (side, 1 - side):
        for piece in pieces:
            to_near(half, piece).wait_send()
            to_far(half, piece).wait_send()


def fused(static_control, alpha_field, perturbations, static_scale, length_x, length_y, lengths):
    groups = lax.axis_size("sub") // 2
    unused, levels, rows, cells = static_control.shape
    variables = perturbations.shape[1]
    width = cells // (2 * PARTS)
    units = 2 * PARTS
    flat = (levels * rows, width)
    anywhere = pl.BlockSpec(memory_space=pl.ANY)
    smem = pl.BlockSpec(memory_space=pltpu.SMEM)

    def buffer(*shape):
        return pltpu.VMEM(shape, jnp.float32)

    dma = pltpu.SemaphoreType.DMA
    out = pl.pallas_call(
        functools.partial(kernel, groups, levels),
        out_shape=jax.ShapeDtypeStruct((levels, rows, cells), jnp.float32),
        in_specs=[anywhere] * 3 + [smem] * 4,
        out_specs=pl.BlockSpec(memory_space=pltpu.VMEM),
        scratch_shapes=[
            buffer(levels, rows, cells),
            buffer(levels, rows, cells),
            pltpu.VMEM((variables, levels * rows, cells), jnp.bfloat16),
            pltpu.VMEM((levels, 2 * BLK, 2 * BLK), jnp.bfloat16),
            pltpu.VMEM((levels, 2 * BLK, 2 * BLK), jnp.bfloat16),
            buffer(units, 2, *flat),
            buffer(units, 2, *flat),
            buffer(units, 2, 4 * levels, width),
            buffer(units, groups - 1, 4 * levels, width),
            buffer(units, *flat),
            buffer(units, 2, *flat),
            buffer(2, PARTS, 2, *flat),
            buffer(2, PARTS, 2, *flat),
            buffer(2, PARTS, *flat),
            buffer(2, PARTS, *flat),
            buffer(2, PARTS, *flat),
            dma((3,)),
            dma((units,)), dma((units,)),
            dma((units, groups)), dma((units, groups)),
            dma((units,)), dma((units,)),
            dma((2, PARTS)), dma((2, PARTS)),
            dma((2, PARTS)), dma((2, PARTS)),
        ],
        compiler_params=pltpu.CompilerParams(
            collective_id=0, has_side_effects=True, vmem_limit_bytes=60 * 1024 * 1024
        ),
    )(
        static_control[0], alpha_field[0],
        perturbations.reshape(variables, levels * rows, cells),
        static_scale, length_x, length_y, lengths,
    )
    return out[None]


def fits(mesh):
    return mesh.shape["sub"] == 8 and mesh.shape["mem"] == 4


def solution(mesh):
    return jax.shard_map(
        fused if fits(mesh) else body,
        mesh=mesh,
        in_specs=(
            P("mem", None, "sub", None),
            P("mem", None, "sub", None),
            P("mem", None, None, "sub", None),
            P("mem", None),
            P(),
            P(),
            P(),
        ),
        out_specs=P("mem", None, "sub", None),
        check_vma=False,
    )
```
